32 devices in a mesh: grid: 8 (over z, core), band: 4 (over y, x).
Axes of the slice: x: 2, y: 2, z: 4, core: 2. Of those that a mesh axis runs over, the one named last changes fastest.
Arguments:
- orbitals: float32 [2048, 8192], P('band', 'grid'), may hold values from -0.6 to 0.6
- points: int32 [1536], replicated, may hold values from 0 to 8191, as said below
Outputs:
- fitted: float32 [8192, 1536], P(('grid', 'band'))
The draws below stay inside these ranges and needn't reach their ends.
Inputs may be any that keep to these rules, and one draw needn't show every extreme that they name: Grid indices of interpolation points; each aligned domain of grid points d * 1024 to (d + 1) * 1024 - 1 holds at least one, the rest cluster unevenly around a few centres; repeats may occur.
All inputs are finite; a program needn't handle non-finite values.
Results may differ from the reference program's by a relative error of at most 0.000092.
Values sent between devices are 32-bit elements; how exact they have to be, the bound alone decides.
A program may use at most 64 MiB of HBM per device.

```python
import jax
import jax.numpy as jnp
from jax import lax

SLAB = 1024
COLS = 1536
BANDS = 2048
NG = 8192


def draw_points(key, part):
    key = jax.random.fold_in(key, 7)
    domains = NG // SLAB
    first_key, centre_key, pick_key, offset_key = jax.random.split(key, 4)
    spread_pts = jax.random.randint(first_key, (domains,), 0, SLAB) + jnp.arange(domains) * SLAB
    spread_pts = spread_pts.at[0].set(0).at[domains - 1].set(NG - 1)
    centres = jax.random.randint(centre_key, (8,), 0, NG)
    rest = COLS - domains
    which = jax.random.randint(pick_key, (rest,), 0, 8)
    offsets = jax.random.randint(offset_key, (rest,), -(SLAB // 2), SLAB // 2 + 1)
    clustered = jnp.mod(centres[which] + offsets, NG)
    return jnp.concatenate([spread_pts, clustered]).astype(jnp.int32)


def levels(stream_key, shape, shards, least, top_value):
    def one(axis_at, shards_of):
        heights = jax.random.uniform(jax.random.fold_in(jax.random.fold_in(stream_key, 6), axis_at), (shards_of,), jnp.float32, least / len(shards), top_value / len(shards))
        return jnp.repeat(jnp.exp(heights), shape[axis_at] // shards_of).reshape((-1,) + (1,) * (len(shape) - axis_at - 1))

    loudness = one(*shards[0])
    for cut in shards[1:]:
        loudness = loudness * one(*cut)
    return loudness


def normal_values(own_key, dims, spread, reach, pieces=(), kind=jnp.bfloat16):
    result = spread * jax.random.normal(own_key, dims, jnp.float32)
    if pieces:
        result = result * levels(own_key, dims, pieces, -0.22, 0.18)
    return jnp.clip(result, -reach, reach).astype(kind)


def setup_inputs(seed: int = 0) -> dict:
    key_of = jax.random.split(jax.random.key(seed), 3)
    return {
        "orbitals": normal_values(key_of[0], (BANDS, NG), 0.105, 0.6, ((0, 4), (1, 8)), jnp.float32),
        "points": draw_points(jax.random.fold_in(key_of[2], 71), 0),
    }


def reference(orbitals, points):
    sampled = jnp.take(orbitals, points, axis=1)
    density = lax.dot_general(orbitals, sampled, (((0,), (0,)), ((), ())), precision=lax.Precision.HIGHEST, preferred_element_type=jnp.float32)
    return density * density
```

```python
import functools

import jax
import jax.numpy as jnp
from jax import lax
from jax.experimental import pallas as pl
from jax.experimental.pallas import tpu as pltpu
from jax.sharding import PartitionSpec as P

WIDTH = 128


def split(x):
    high = x.astype(jnp.bfloat16)
    return high, (x - high.astype(jnp.float32)).astype(jnp.bfloat16)


def dot(a, b):
    return lax.dot_general(a, b, (((1,), (0,)), ((), ())), preferred_element_type=jnp.float32)


def kernel(
    chips, group, bits,
    orb_ref, pts_ref, out_ref,
    halves, turned, turned_hi, turned_lo,
    own, sibs, came, incl, sib_incl, acc, *rest,
):
    got, sems = rest[:bits], rest[bits:]
    own_s, own_r, came_s, came_r, incl_s, incl_r, red_s, red_r = sems
    bands, slab = orb_ref.shape
    chunks = pts_ref.shape[0]
    rows = slab // group
    g, b = lax.axis_index("grid"), lax.axis_index("band")
    z, core = g // 2, g % 2
    toward = 1 - 2 * core
    pos = z * (1 - core) + (chips - 1 - z) * core
    sibling = g + toward
    after, before = g + 2 * toward, g - 2 * toward
    first, last = pos == 0, pos == chips - 1
    flip = [(1 - 2 * ((b // 2**k) % 2)) * 2**k for k in range(bits)]

    def partner(chunk, stage):
        k = (chunk + stage) % bits
        return b + sum((k == i).astype(jnp.int32) * flip[i] for i in range(bits))

    barrier = pltpu.get_barrier_semaphore()

    def greet(to_g, to_b):
        pl.semaphore_signal(barrier, inc=1, device_id=(to_g, to_b), device_id_type=pl.DeviceIdType.MESH)

    greet(sibling, b)
    for k in range(bits):
        greet(g, b + flip[k])

    @pl.when(pos > 0)
    def _():
        greet(before, b)

    @pl.when(pos < chips - 1)
    def _():
        greet(after, b)

    def remote(src, dst, send, recv, to_g, to_b):
        return pltpu.make_async_remote_copy(
            src_ref=src, dst_ref=dst, send_sem=send, recv_sem=recv,
            device_id=(to_g, to_b), device_id_type=pl.DeviceIdType.MESH,
        )

    def own_copy(t):
        return remote(own.at[t], sibs.at[t], own_s.at[t], own_r.at[t], sibling, b)

    def chain_copy(t):
        return remote(incl.at[t], came.at[t], came_s.at[t], came_r.at[t], after, b)

    def incl_copy(t):
        return remote(incl.at[t], sib_incl.at[t], incl_s.at[t], incl_r.at[t], sibling, b)

    def reduce_copy(t, stage):
        size = slab >> (stage + 1)
        return remote(
            acc.at[t, pl.ds(size, size)], got[stage].at[t],
            red_s.at[stage, t], red_r.at[stage, t], g, partner(t, stage),
        )

    def pick(t):
        where = pts_ref[t] - g * slab
        hot = lax.broadcasted_iota(jnp.int32, (slab, WIDTH), 0) == where
        both = dot(halves[...], jnp.where(hot, 1.0, 0.0).astype(jnp.bfloat16))
        own[t] = both[:bands] + both[bands:]

    def turn():
        turned[...] = orb_ref[...].T
        for turn_by in range(bits):
            for slot in range(group):
                block = b
                for j in range(bits):
                    if slot & (group >> (j + 1)):
                        block = block + flip[(turn_by + j) % bits]
                high, low = split(turned[pl.ds(pl.multiple_of(block * rows, rows), rows), :])
                turned_hi[turn_by, slot * rows:(slot + 1) * rows, :] = high
                turned_lo[turn_by, slot * rows:(slot + 1) * rows, :] = low

    def forward(t):
        own_copy(t).wait_recv()

        @pl.when(first)
        def _():
            came[t] = jnp.zeros((bands, WIDTH), jnp.float32)

        @pl.when(jnp.logical_not(first))
        def _():
            chain_copy(t).wait_recv()

        incl[t] = came[t] + own[t] + sibs[t]

        @pl.when(jnp.logical_not(last))
        def _():
            chain_copy(t).start()

        incl_copy(t).start()

    def contract(t):
        incl_copy(t).wait_recv()
        high, low = split(came[t] + sib_incl[t])
        pair = jnp.concatenate([high, low], axis=1)
        by = t % bits
        half = slab // 2

        def part(at):
            two = dot(turned_hi[by, at:at + half, :], pair)
            acc[t, at:at + half, :] = two[:, :WIDTH] + two[:, WIDTH:] + dot(turned_lo[by, at:at + half, :], high)

        part(half)
        reduce_copy(t, 0).start()
        part(0)

    def add(t, stage):
        size = slab >> (stage + 1)
        reduce_copy(t, stage).wait_recv()
        if stage + 1 < bits:
            less = size // 2
            acc[t, less:size, :] += got[stage][t, less:, :]
            reduce_copy(t, stage + 1).start()
            acc[t, :less, :] += got[stage][t, :less, :]
        else:
            out_ref[:, pl.ds(pl.multiple_of(t * WIDTH, WIDTH), WIDTH)] = acc[t, :size, :] + got[stage][t]

    high, low = split(orb_ref[...])
    halves[:bands, :] = high
    halves[bands:, :] = low
    pick(0)
    pl.semaphore_wait(barrier, 1 + bits + (pos > 0).astype(jnp.int32) + (pos < chips - 1).astype(jnp.int32))
    own_copy(0).start()

    behind = chips - 1

    def step(s, carry):
        @pl.when(s + 1 < chunks)
        def _():
            pick(s + 1)
            own_copy(s + 1).start()

        f = s - pos

        @pl.when(jnp.logical_and(f >= 0, f < chunks))
        def _():
            forward(f)

        @pl.when(s == 0)
        def _():
            turn()

        c = s - behind

        @pl.when(jnp.logical_and(c >= 0, c < chunks))
        def _():
            contract(c)

        for stage in range(bits):
            r = c - 2 * (stage + 1)

            @pl.when(jnp.logical_and(r >= 0, r < chunks))
            def _(r=r, stage=stage):
                add(r, stage)

        return carry

    lax.fori_loop(0, chunks + behind + 2 * bits, step, 0)

    def drain(t, carry):
        own_copy(t).wait_send()

        @pl.when(jnp.logical_not(last))
        def _():
            chain_copy(t).wait_send()

        incl_copy(t).wait_send()
        for stage in range(bits):
            reduce_copy(t, stage).wait_send()
        return carry

    lax.fori_loop(0, chunks, drain, 0)


def shards(sizes, orbitals, points):
    grid, group = sizes
    bits = group.bit_length() - 1
    bands, slab = orbitals.shape
    columns = points.shape[0]
    chunks = columns // WIDTH
    rows = slab // group
    piece = (chunks, bands, WIDTH)
    dma = pltpu.SemaphoreType.DMA
    density = pl.pallas_call(
        functools.partial(kernel, grid // 2, group, bits),
        out_shape=jax.ShapeDtypeStruct((rows, columns), jnp.float32),
        in_specs=[pl.BlockSpec(memory_space=pltpu.VMEM)] * 2,
        out_specs=pl.BlockSpec(memory_space=pltpu.VMEM),
        scratch_shapes=[
            pltpu.VMEM((2 * bands, slab), jnp.bfloat16),
            pltpu.VMEM((slab, bands), jnp.float32),
            pltpu.VMEM((bits, slab, bands), jnp.bfloat16),
            pltpu.VMEM((bits, slab, bands), jnp.bfloat16),
            *[pltpu.VMEM(piece, jnp.float32) for _ in range(5)],
            pltpu.VMEM((chunks, slab, WIDTH), jnp.float32),
            *[pltpu.VMEM((chunks, slab >> (j + 1), WIDTH), jnp.float32) for j in range(bits)],
            *[dma((chunks,)) for _ in range(6)],
            dma((bits, chunks)),
            dma((bits, chunks)),
        ],
        compiler_params=pltpu.CompilerParams(
            collective_id=0, has_side_effects=True, vmem_limit_bytes=60 * 2**20
        ),
        cost_estimate=pl.CostEstimate(
            flops=10 * bands * slab * columns, bytes_accessed=8 * bands * slab, transcendentals=0
        ),
    )(orbitals, points.reshape(chunks, 1, WIDTH))
    return density * density


def solution(mesh):
    sizes = (mesh.shape["grid"], mesh.shape["band"])
    return jax.shard_map(
        functools.partial(shards, sizes),
        mesh=mesh,
        in_specs=(P("band", "grid"), P()),
        out_specs=P(("grid", "band"), None),
        check_vma=False,
    )
```

```python
import functools

import jax
import jax.numpy as jnp
from jax import lax
from jax.experimental import pallas as pl
from jax.experimental.pallas import tpu as pltpu
from jax.sharding import PartitionSpec as P

WIDTH = 128
PIECES = 4
LAG = 2


def split(x):
    high = x.astype(jnp.bfloat16)
    return high, (x - high.astype(jnp.float32)).astype(jnp.bfloat16)


def dot(a, b):
    return lax.dot_general(a, b, (((1,), (0,)), ((), ())), preferred_element_type=jnp.float32)


def kernel(
    chips, group, bits,
    orb_ref, pts_ref, out_ref,
    halves, turned, turned_hi, turned_lo,
    own, sibs, came, incl, sib_incl, acc, *rest,
):
    got, sems = rest[:bits], rest[bits:]
    own_s, own_r, came_s, came_r, incl_s, incl_r, red_s, red_r = sems
    bands, slab = orb_ref.shape
    chunks = pts_ref.shape[0] // WIDTH
    rows = slab // group
    g, b = lax.axis_index("grid"), lax.axis_index("band")
    z, core = g // 2, g % 2
    toward = 1 - 2 * core
    pos = z * (1 - core) + (chips - 1 - z) * core
    sibling = g + toward
    after, before = g + 2 * toward, g - 2 * toward
    first, last = pos == 0, pos == chips - 1
    flip = [(1 - 2 * ((b // 2**k) % 2)) * 2**k for k in range(bits)]

    def partner(chunk, stage):
        k = (chunk + core + stage) % bits
        return b + sum((k == i).astype(jnp.int32) * flip[i] for i in range(bits))

    barrier = pltpu.get_barrier_semaphore()

    def greet(to_g, to_b):
        pl.semaphore_signal(barrier, inc=1, device_id=(to_g, to_b), device_id_type=pl.DeviceIdType.MESH)

    greet(sibling, b)
    for k in range(bits):
        greet(g, b + flip[k])

    @pl.when(pos > 0)
    def _():
        greet(before, b)

    @pl.when(pos < chips - 1)
    def _():
        greet(after, b)

    def remote(src, dst, send, recv, to_g, to_b):
        return pltpu.make_async_remote_copy(
            src_ref=src, dst_ref=dst, send_sem=send, recv_sem=recv,
            device_id=(to_g, to_b), device_id_type=pl.DeviceIdType.MESH,
        )

    def own_copy(t):
        return remote(own.at[t], sibs.at[t], own_s.at[t], own_r.at[t], sibling, b)

    def chain_copy(t, p):
        size = bands // PIECES
        at = pl.ds(p * size, size)
        return remote(incl.at[t, at], came.at[t, at], came_s.at[p, t], came_r.at[p, t], after, b)

    def incl_copy(t):
        return remote(incl.at[t], sib_incl.at[t], incl_s.at[t], incl_r.at[t], sibling, b)

    def parts(stage):
        return (1, 0) if stage + 1 < bits else (0,)

    def reduce_copy(t, stage, part):
        size = slab >> (stage + 1)
        each = size // len(parts(stage))
        return remote(
            acc.at[t, pl.ds(size + part * each, each)], got[stage].at[t, pl.ds(part * each, each)],
            red_s.at[stage, part, t], red_r.at[stage, part, t], g, partner(t, stage),
        )

    def pick(t):
        where = (pts_ref[pl.ds(pl.multiple_of(t * WIDTH, WIDTH), WIDTH)] - g * slab)[None, :]
        hot = lax.broadcasted_iota(jnp.int32, (slab, WIDTH), 0) == where
        both = dot(halves[...], jnp.where(hot, 1.0, 0.0).astype(jnp.bfloat16))
        own[t] = both[:bands] + both[bands:]

    def turn():
        turned[...] = orb_ref[...].T
        for turn_by in range(bits):
            for slot in range(group):
                block = b
                for j in range(bits):
                    if slot & (group >> (j + 1)):
                        block = block + flip[(turn_by + j) % bits]
                high, low = split(turned[pl.ds(pl.multiple_of(block * rows, rows), rows), :])
                turned_hi[turn_by, slot * rows:(slot + 1) * rows, :] = high
                turned_lo[turn_by, slot * rows:(slot + 1) * rows, :] = low

    def forward(t):
        own_copy(t).wait_recv()

        @pl.when(first)
        def _():
            came[t] = jnp.zeros((bands, WIDTH), jnp.float32)

        for p in range(PIECES):
            size = bands // PIECES
            at = pl.ds(p * size, size)

            @pl.when(jnp.logical_not(first))
            def _(p=p):
                chain_copy(t, p).wait_recv()

            incl[t, at] = came[t, at] + own[t, at] + sibs[t, at]

            @pl.when(jnp.logical_not(last))
            def _(p=p):
                chain_copy(t, p).start()

        incl_copy(t).start()

    def contract(t):
        incl_copy(t).wait_recv()
        high, low = split(came[t] + sib_incl[t])
        pair = jnp.concatenate([high, low], axis=1)
        by = (t + core) % bits
        half = slab // 2

        def part(at):
            two = dot(turned_hi[by, at:at + half, :], pair)
            acc[t, at:at + half, :] = two[:, :WIDTH] + two[:, WIDTH:] + dot(turned_lo[by, at:at + half, :], high)

        part(half)
        for p in parts(0):
            reduce_copy(t, 0, p).start()
        part(0)

    def add(t, stage):
        size = slab >> (stage + 1)
        if stage > 0:
            reduce_copy(t, stage - 1, 0).wait_recv()
            acc[t, :size, :] += got[stage - 1][t, :size, :]
        if stage + 1 < bits:
            less = size // 2
            reduce_copy(t, stage, 1).wait_recv()
            acc[t, less:size, :] += got[stage][t, less:, :]
            for p in parts(stage + 1):
                reduce_copy(t, stage + 1, p).start()
        else:
            reduce_copy(t, stage, 0).wait_recv()
            out_ref[:, pl.ds(pl.multiple_of(t * WIDTH, WIDTH), WIDTH)] = acc[t, :size, :] + got[stage][t]

    high, low = split(orb_ref[...])
    halves[:bands, :] = high
    halves[bands:, :] = low
    pick(0)
    pl.semaphore_wait(barrier, 1 + bits + (pos > 0).astype(jnp.int32) + (pos < chips - 1).astype(jnp.int32))
    own_copy(0).start()

    behind = chips - 1

    def step(s, carry):
        @pl.when(s + 1 < chunks)
        def _():
            pick(s + 1)
            own_copy(s + 1).start()

        f = s - pos

        @pl.when(jnp.logical_and(f >= 0, f < chunks))
        def _():
            forward(f)

        @pl.when(s == 0)
        def _():
            turn()

        c = s - behind

        @pl.when(jnp.logical_and(c >= 0, c < chunks))
        def _():
            contract(c)

        for stage in range(bits):
            r = c - LAG * (stage + 1)

            @pl.when(jnp.logical_and(r >= 0, r < chunks))
            def _(r=r, stage=stage):
                add(r, stage)

        return carry

    lax.fori_loop(0, chunks + behind + LAG * bits, step, 0)

    def drain(t, carry):
        own_copy(t).wait_send()

        @pl.when(jnp.logical_not(last))
        def _():
            for p in range(PIECES):
                chain_copy(t, p).wait_send()

        incl_copy(t).wait_send()
        for stage in range(bits):
            for p in parts(stage):
                reduce_copy(t, stage, p).wait_send()
        return carry

    lax.fori_loop(0, chunks, drain, 0)


def shards(sizes, orbitals, points):
    grid, group = sizes
    bits = group.bit_length() - 1
    bands, slab = orbitals.shape
    columns = points.shape[0]
    chunks = columns // WIDTH
    rows = slab // group
    piece = (chunks, bands, WIDTH)
    dma = pltpu.SemaphoreType.DMA
    density = pl.pallas_call(
        functools.partial(kernel, grid // 2, group, bits),
        out_shape=jax.ShapeDtypeStruct((rows, columns), jnp.float32),
        in_specs=[pl.BlockSpec(memory_space=pltpu.VMEM)] * 2,
        out_specs=pl.BlockSpec(memory_space=pltpu.VMEM),
        scratch_shapes=[
            pltpu.VMEM((2 * bands, slab), jnp.bfloat16),
            pltpu.VMEM((slab, bands), jnp.float32),
            pltpu.VMEM((bits, slab, bands), jnp.bfloat16),
            pltpu.VMEM((bits, slab, bands), jnp.bfloat16),
            *[pltpu.VMEM(piece, jnp.float32) for _ in range(5)],
            pltpu.VMEM((chunks, slab, WIDTH), jnp.float32),
            *[pltpu.VMEM((chunks, slab >> (j + 1), WIDTH), jnp.float32) for j in range(bits)],
            dma((chunks,)),
            dma((chunks,)),
            dma((PIECES, chunks)),
            dma((PIECES, chunks)),
            dma((chunks,)),
            dma((chunks,)),
            dma((bits, 2, chunks)),
            dma((bits, 2, chunks)),
        ],
        compiler_params=pltpu.CompilerParams(
            collective_id=0, has_side_effects=True, vmem_limit_bytes=44 * 2**20
        ),
        cost_estimate=pl.CostEstimate(
            flops=10 * bands * slab * columns, bytes_accessed=8 * bands * slab, transcendentals=0
        ),
    )(orbitals, points)
    return density * density


def solution(mesh):
    sizes = (mesh.shape["grid"], mesh.shape["band"])
    return jax.shard_map(
        functools.partial(shards, sizes),
        mesh=mesh,
        in_specs=(P("band", "grid"), P()),
        out_specs=P(("grid", "band"), None),
        check_vma=False,
    )
```

```python
import functools

import jax
import jax.numpy as jnp
from jax import lax
from jax.experimental import pallas as pl
from jax.experimental.pallas import tpu as pltpu
from jax.sharding import PartitionSpec as P

WIDTH = 128
PIECES = 4
LAG = 2
REST = 2


def split(x):
    high = x.astype(jnp.bfloat16)
    return high, (x - high.astype(jnp.float32)).astype(jnp.bfloat16)


def dot(a, b):
    return lax.dot_general(a, b, (((1,), (0,)), ((), ())), preferred_element_type=jnp.float32)


def kernel(
    chips, group, bits,
    orb_ref, pts_ref, out_ref,
    halves, turned, turned_hi, turned_lo,
    own, sibs, came, incl, sib_incl, acc, *rest,
):
    got, sems = rest[:bits], rest[bits:]
    own_s, own_r, came_s, came_r, incl_s, incl_r, red_s, red_r = sems
    bands, slab = orb_ref.shape
    chunks = pts_ref.shape[0] // WIDTH
    rows = slab // group
    g, b = lax.axis_index("grid"), lax.axis_index("band")
    z, core = g // 2, g % 2
    toward = 1 - 2 * core
    pos = z * (1 - core) + (chips - 1 - z) * core
    sibling = g + toward
    after, before = g + 2 * toward, g - 2 * toward
    first, last = pos == 0, pos == chips - 1
    flip = [(1 - 2 * ((b // 2**k) % 2)) * 2**k for k in range(bits)]

    def partner(chunk, stage):
        k = (chunk + core + stage) % bits
        return b + sum((k == i).astype(jnp.int32) * flip[i] for i in range(bits))

    barrier = pltpu.get_barrier_semaphore()

    def greet(to_g, to_b):
        pl.semaphore_signal(barrier, inc=1, device_id=(to_g, to_b), device_id_type=pl.DeviceIdType.MESH)

    greet(sibling, b)
    for k in range(bits):
        greet(g, b + flip[k])

    @pl.when(pos > 0)
    def _():
        greet(before, b)

    @pl.when(pos < chips - 1)
    def _():
        greet(after, b)

    def remote(src, dst, send, recv, to_g, to_b):
        return pltpu.make_async_remote_copy(
            src_ref=src, dst_ref=dst, send_sem=send, recv_sem=recv,
            device_id=(to_g, to_b), device_id_type=pl.DeviceIdType.MESH,
        )

    def own_copy(t):
        return remote(own.at[t], sibs.at[t], own_s.at[t], own_r.at[t], sibling, b)

    def chain_copy(t, p):
        size = bands // PIECES
        at = pl.ds(p * size, size)
        return remote(incl.at[t, at], came.at[t, at], came_s.at[p, t], came_r.at[p, t], after, b)

    def incl_copy(t):
        return remote(incl.at[t], sib_incl.at[t], incl_s.at[t], incl_r.at[t], sibling, b)

    def parts(stage):
        return (1, 0) if stage + 1 < bits else (0,)

    def reduce_copy(t, stage, part):
        size = slab >> (stage + 1)
        each = size // len(parts(stage))
        return remote(
            acc.at[t, pl.ds(size + part * each, each)], got[stage].at[t, pl.ds(part * each, each)],
            red_s.at[stage, part, t], red_r.at[stage, part, t], g, partner(t, stage),
        )

    def pick(t):
        where = (pts_ref[pl.ds(pl.multiple_of(t * WIDTH, WIDTH), WIDTH)] - g * slab)[None, :]
        hot = lax.broadcasted_iota(jnp.int32, (slab, WIDTH), 0) == where
        both = dot(halves[...], jnp.where(hot, 1.0, 0.0).astype(jnp.bfloat16))
        own[t] = both[:bands] + both[bands:]

    def turn():
        turned[...] = orb_ref[...].T
        for turn_by in range(bits):
            for slot in range(group):
                block = b
                for j in range(bits):
                    if slot & (group >> (j + 1)):
                        block = block + flip[(turn_by + j) % bits]
                high, low = split(turned[pl.ds(pl.multiple_of(block * rows, rows), rows), :])
                turned_hi[turn_by, slot * rows:(slot + 1) * rows, :] = high
                turned_lo[turn_by, slot * rows:(slot + 1) * rows, :] = low

    def forward(t):
        own_copy(t).wait_recv()

        @pl.when(first)
        def _():
            came[t] = jnp.zeros((bands, WIDTH), jnp.float32)

        for p in range(PIECES):
            size = bands // PIECES
            at = pl.ds(p * size, size)

            @pl.when(jnp.logical_not(first))
            def _(p=p):
                chain_copy(t, p).wait_recv()

            incl[t, at] = came[t, at] + own[t, at] + sibs[t, at]

            @pl.when(jnp.logical_not(last))
            def _(p=p):
                chain_copy(t, p).start()

        incl_copy(t).start()

    def contract(t):
        incl_copy(t).wait_recv()
        high, low = split(came[t] + sib_incl[t])
        pair = jnp.concatenate([high, low], axis=1)
        by = (t + core) % bits
        half = slab // 2

        def part(at):
            two = dot(turned_hi[by, at:at + half, :], pair)
            acc[t, at:at + half, :] = two[:, :WIDTH] + two[:, WIDTH:] + dot(turned_lo[by, at:at + half, :], high)

        part(half)
        for p in parts(0):
            reduce_copy(t, 0, p).start()
        part(0)

    def add(t, stage):
        size = slab >> (stage + 1)
        if stage > 0:
            reduce_copy(t, stage - 1, 0).wait_recv()
            acc[t, :size, :] += got[stage - 1][t, :size, :]
        if stage + 1 < bits:
            less = size // 2
            reduce_copy(t, stage, 1).wait_recv()
            acc[t, less:size, :] += got[stage][t, less:, :]
            for p in parts(stage + 1):
                reduce_copy(t, stage + 1, p).start()
        else:
            reduce_copy(t, stage, 0).wait_recv()
            out_ref[:, pl.ds(pl.multiple_of(t * WIDTH, WIDTH), WIDTH)] = acc[t, :size, :] + got[stage][t]

    high, low = split(orb_ref[...])
    halves[:bands, :] = high
    halves[bands:, :] = low
    pick(0)
    pl.semaphore_wait(barrier, 1 + bits + (pos > 0).astype(jnp.int32) + (pos < chips - 1).astype(jnp.int32))
    own_copy(0).start()

    behind = chips - 1

    def step(s, carry):
        @pl.when(s + 1 < chunks)
        def _():
            pick(s + 1)
            own_copy(s + 1).start()

        f = s - pos

        @pl.when(jnp.logical_and(f >= 0, f < chunks))
        def _():
            forward(f)

        @pl.when(s == 0)
        def _():
            turn()

        c = s - behind

        @pl.when(jnp.logical_and(c >= 0, c < chunks))
        def _():
            contract(c)

        for stage in range(bits):
            r = c - LAG * (stage + 1) - (REST if stage + 1 == bits else 0)

            @pl.when(jnp.logical_and(r >= 0, r < chunks))
            def _(r=r, stage=stage):
                add(r, stage)

        return carry

    lax.fori_loop(0, chunks + behind + LAG * bits + REST, step, 0)

    def drain(t, carry):
        own_copy(t).wait_send()

        @pl.when(jnp.logical_not(last))
        def _():
            for p in range(PIECES):
                chain_copy(t, p).wait_send()

        incl_copy(t).wait_send()
        for stage in range(bits):
            for p in parts(stage):
                reduce_copy(t, stage, p).wait_send()
        return carry

    lax.fori_loop(0, chunks, drain, 0)


def shards(sizes, orbitals, points):
    grid, group = sizes
    bits = group.bit_length() - 1
    bands, slab = orbitals.shape
    columns = points.shape[0]
    chunks = columns // WIDTH
    rows = slab // group
    piece = (chunks, bands, WIDTH)
    dma = pltpu.SemaphoreType.DMA
    density = pl.pallas_call(
        functools.partial(kernel, grid // 2, group, bits),
        out_shape=jax.ShapeDtypeStruct((rows, columns), jnp.float32),
        in_specs=[pl.BlockSpec(memory_space=pltpu.VMEM)] * 2,
        out_specs=pl.BlockSpec(memory_space=pltpu.VMEM),
        scratch_shapes=[
            pltpu.VMEM((2 * bands, slab), jnp.bfloat16),
            pltpu.VMEM((slab, bands), jnp.float32),
            pltpu.VMEM((bits, slab, bands), jnp.bfloat16),
            pltpu.VMEM((bits, slab, bands), jnp.bfloat16),
            *[pltpu.VMEM(piece, jnp.float32) for _ in range(5)],
            pltpu.VMEM((chunks, slab, WIDTH), jnp.float32),
            *[pltpu.VMEM((chunks, slab >> (j + 1), WIDTH), jnp.float32) for j in range(bits)],
            dma((chunks,)),
            dma((chunks,)),
            dma((PIECES, chunks)),
            dma((PIECES, chunks)),
            dma((chunks,)),
            dma((chunks,)),
            dma((bits, 2, chunks)),
            dma((bits, 2, chunks)),
        ],
        compiler_params=pltpu.CompilerParams(
            collective_id=0, has_side_effects=True, vmem_limit_bytes=44 * 2**20
        ),
        cost_estimate=pl.CostEstimate(
            flops=10 * bands * slab * columns, bytes_accessed=8 * bands * slab, transcendentals=0
        ),
    )(orbitals, points)
    return density * density


def solution(mesh):
    sizes = (mesh.shape["grid"], mesh.shape["band"])
    return jax.shard_map(
        functools.partial(shards, sizes),
        mesh=mesh,
        in_specs=(P("band", "grid"), P()),
        out_specs=P(("grid", "band"), None),
        check_vma=False,
    )
```
